512 devices in a mesh: pipe: 16 (over y, x), expert: 32 (over z, core).
Axes of the slice: x: 4, y: 4, z: 16, core: 2. Of those that a mesh axis runs over, the one named last changes fastest.
Arguments:
- token_rows: bfloat16 [8192, 7168], P('expert', 'pipe'), may hold values from -6 to 6
- row_scale: bfloat16 [8192], P('expert'), may hold values from 0.25 to 4
- routes: int32 [8192, 8], P('expert'), may hold values from 0 to 255, as said below
- gate_weights: bfloat16 [8192, 8], P('expert'), may hold values from 0.049804688 to 0.59765625
- up_weight: bfloat16 [32, 7168, 2048], P('expert', 'pipe'), may hold values from -0.0625 to 0.0625
- down_weight: bfloat16 [32, 2048, 7168], P('expert', None, 'pipe'), may hold values from -0.125 to 0.125
Outputs:
- combined: float32 [8192, 7168], P('expert', 'pipe')
The draws below stay inside these ranges and needn't reach their ends.
Inputs may be any that keep to these rules, and one draw needn't show every extreme that they name: `routes`: A token names 8 different experts. Among the 256 tokens of one index of expert, no expert below 32 is named by more than 16 of them, and in every draw one expert below 32 is named by exactly 16 tokens of every index of expert.
All inputs are finite; a program needn't handle non-finite values.
Results may differ from the reference program's by a relative error of at most 0.004.
Values may be sent and summed in bfloat16 or wider, within the bound.
No kernel may reach another device: no remote copies, remote signals or barrier semaphores. Data moves between devices by JAX's collectives and lax.ppermute only.
A program may use at most 64 MiB of HBM per device.

```python
import math
import jax
import jax.numpy as jnp
from jax import lax

D = 7168
FF = 2048
TOPK = 8
EXPERTS_ALL = 256
EXPERT_TOKENS = 256
EXPERTS = 32
TOKENS = 8192
CAP = 16
N_EXPERT = 32


def draw_routes(key, part):
    key = jax.random.fold_in(key, 11)
    star_key, block_key = jax.random.split(key)
    star = jax.random.randint(star_key, (), 0, EXPERTS)
    outside = EXPERTS_ALL - EXPERTS
    stride = outside // TOPK
    slot_index = jnp.arange(EXPERTS * CAP, dtype=jnp.int32)
    expert_ids = jnp.arange(EXPERTS, dtype=jnp.int32)
    member_ranks = jnp.arange(TOPK, dtype=jnp.int32)

    def one_block(subkey):
        keys = jax.random.split(subkey, 5)
        shifts = jax.random.randint(keys[0], (EXPERTS,), 0, 4)
        counts = jnp.maximum(CAP // jnp.left_shift(jnp.int32(1), shifts), 1)
        second = jax.random.randint(keys[1], (), 0, EXPERTS)
        counts = jnp.where((expert_ids == star) | (expert_ids == second), CAP, counts).astype(jnp.int32)
        ends = jnp.cumsum(counts)
        filled = ends[-1]
        owning_member = jnp.sum((slot_index[:, None] >= ends[None, :]).astype(jnp.int32), axis=1)
        order = jax.random.permutation(keys[2], EXPERT_TOKENS).astype(jnp.int32)
        holding_member = order[slot_index % EXPERT_TOKENS]
        column_slot = jnp.where(slot_index < filled, slot_index // EXPERT_TOKENS, 2)
        travelling_rows = jnp.full((EXPERT_TOKENS, 2), -1, jnp.int32).at[holding_member, column_slot].set(owning_member, mode='drop')
        held_rows = jnp.sum((travelling_rows >= 0).astype(jnp.int32), axis=1)
        base = jax.random.randint(keys[3], (EXPERT_TOKENS,), 0, outside).at[0].set(outside - 1)
        outer = EXPERTS + (base[:, None] + (member_ranks[None, :] - held_rows[:, None]) * stride) % outside
        inner_loop = jnp.where(member_ranks[None, :] == 0, travelling_rows[:, 0:1], travelling_rows[:, 1:2])
        listed = jnp.where(member_ranks[None, :] < held_rows[:, None], inner_loop, outer)
        turn = jax.random.randint(keys[4], (EXPERT_TOKENS, 1), 0, TOPK)
        index = (member_ranks[None, :] + turn) % TOPK
        return jnp.take_along_axis(listed, index, axis=1)
    blocks = jax.vmap(one_block)(jax.random.split(block_key, TOKENS // EXPERT_TOKENS))
    return blocks.reshape(TOKENS, TOPK).astype(jnp.int32)


def levels(stream_key, extent, cuts, smallest, high):
    loudness, own = 1.0, jax.random.fold_in(stream_key, 6)
    for position, parts in cuts:
        draws = jnp.exp(jax.random.uniform(jax.random.fold_in(own, position), (parts,), jnp.float32, smallest / len(cuts), high / len(cuts)))
        loudness = loudness * jnp.repeat(draws, extent[position] // parts).reshape([-1 if axis == position else 1 for axis in range(len(extent))])
    return loudness


def bell_draw(own_key, dims, width, reach, cuts=(), kind=jnp.bfloat16):
    level = levels(own_key, dims, cuts, -0.22, 0.18) if cuts else 1.0
    result = jax.random.normal(own_key, dims, jnp.float32) * width * level
    return jnp.minimum(jnp.maximum(result, -reach), reach).astype(kind)


def setup_inputs(seed: int = 0) -> dict:
    arg_keys = jax.random.split(jax.random.key(seed), 7)
    return {
        "token_rows": bell_draw(arg_keys[0], (TOKENS, D), 1.0, 6.0, ((0, 32), (1, 16))),
        "row_scale": jnp.clip(jnp.exp(math.log(4.0) - 2.7725887 * jax.random.uniform(arg_keys[1], (TOKENS,), jnp.float32) ** levels(arg_keys[1], (TOKENS,), ((0, 32),), -0.2, 0.2)), 0.25, 4.0).astype(jnp.bfloat16),
        "routes": draw_routes(jax.random.fold_in(arg_keys[6], 71), 0),
        "gate_weights": jnp.clip(jnp.exp(math.log(0.59765625) - 2.4849066 * jax.random.uniform(arg_keys[3], (TOKENS, TOPK), jnp.float32) ** levels(arg_keys[3], (TOKENS, TOPK), ((0, 32),), -0.2, 0.2)), 0.049804688, 0.59765625).astype(jnp.bfloat16),
        "up_weight": bell_draw(arg_keys[4], (EXPERTS, D, FF), D ** -0.5, 0.0625, ((0, 32), (1, 16))),
        "down_weight": bell_draw(arg_keys[5], (EXPERTS, FF, D), FF ** -0.5, 0.125, ((0, 32), (2, 16))),
    }


def reference(token_rows, row_scale, routes, gate_weights, up_weight, down_weight):
    scales = row_scale.astype(jnp.float32)
    gates = gate_weights.astype(jnp.float32)
    slot_count = N_EXPERT * CAP

    def one_expert(running, expert):
        matches = routes == expert
        weight = jnp.sum(jnp.where(matches, gates, jnp.float32(0.0)), axis=1)
        picked = jnp.any(matches, axis=1)
        where_rows = jnp.nonzero(picked, size=slot_count, fill_value=0)[0].astype(jnp.int32)
        filled = jnp.arange(slot_count, dtype=jnp.int32) < jnp.sum(picked.astype(jnp.int32))
        preact = jnp.dot(token_rows[where_rows], up_weight[expert], preferred_element_type=jnp.float32)
        preact = preact * scales[where_rows][:, None]
        active = jax.nn.silu(preact).astype(jnp.bfloat16)
        pieces = jnp.dot(active, down_weight[expert], preferred_element_type=jnp.float32).astype(jnp.bfloat16)
        factor = jnp.where(filled, weight[where_rows], jnp.float32(0.0))
        return running.at[where_rows].add(pieces.astype(jnp.float32) * factor[:, None]), None

    start_sum = jnp.zeros((TOKENS, D), jnp.float32)
    return lax.scan(one_expert, start_sum, jnp.arange(EXPERTS, dtype=jnp.int32))[0]
```

```python
import functools

import jax
import jax.numpy as jnp
from jax import lax
from jax.experimental import pallas as pl
from jax.experimental.pallas import tpu as pltpu
from jax.sharding import PartitionSpec as P

F32 = jnp.float32
BF16 = jnp.bfloat16
WIRE = jnp.float16
WIRE_GAIN = 64.0
NT = (((1,), (1,)), ((), ()))
NN = (((1,), (0,)), ((), ()))
TN = (((0,), (0,)), ((), ()))
VMEM_LIMIT = 40 * 1024 * 1024


def vmem_spec():
    return pl.BlockSpec(memory_space=pltpu.VMEM)


def slot_hits(routes_t, experts, capacity):
    tokens = routes_t.shape[1]
    slots = experts * capacity
    expert_id = lax.broadcasted_iota(jnp.int32, (experts, tokens), 0)
    hot = jnp.zeros((experts, tokens), jnp.bool_)
    for k in range(routes_t.shape[0]):
        hot = hot | (routes_t[k : k + 1, :] == expert_id)
    hot_f = jnp.where(hot, 1.0, 0.0)
    before = lax.broadcasted_iota(jnp.int32, (tokens, tokens), 0) < lax.broadcasted_iota(
        jnp.int32, (tokens, tokens), 1
    )
    rank = lax.dot_general(
        hot_f.astype(BF16),
        jnp.where(before, 1.0, 0.0).astype(BF16),
        NN,
        preferred_element_type=F32,
    )
    rank = jnp.where(hot, rank, -1.0)
    rank_slots = jnp.broadcast_to(rank[:, None, :], (experts, capacity, tokens)).reshape(
        slots, tokens
    )
    place = (lax.broadcasted_iota(jnp.int32, (slots, tokens), 0) % capacity).astype(F32)
    return rank_slots == place


def pick_kernel(experts, capacity, rows_ref, scale_ref, routes_ref, out_ref):
    width = rows_ref.shape[0]
    hits = jnp.where(slot_hits(routes_ref[...], experts, capacity), 1.0, 0.0)
    picked = lax.dot_general(hits.astype(BF16), rows_ref[...], NT, preferred_element_type=F32)
    scale = jnp.sum(hits * scale_ref[...].astype(F32), axis=1, keepdims=True)
    out_ref[:, :width] = picked.astype(BF16)
    out_ref[:, width:] = jnp.broadcast_to(
        scale.astype(BF16), (out_ref.shape[0], out_ref.shape[1] - width)
    )


def gate_kernel(experts, capacity, routes_ref, gate_ref, out_ref):
    routes_t = routes_ref[...]
    tokens = routes_t.shape[1]
    expert_id = lax.broadcasted_iota(jnp.int32, (experts, tokens), 0)
    gate = jnp.zeros((experts, tokens), F32)
    for k in range(routes_t.shape[0]):
        gate = jnp.where(
            routes_t[k : k + 1, :] == expert_id, gate_ref[k : k + 1, :].astype(F32), gate
        )
    gate_slots = jnp.broadcast_to(gate[:, None, :], (experts, capacity, tokens)).reshape(
        experts * capacity, tokens
    )
    hits = slot_hits(routes_t, experts, capacity)
    out_ref[...] = jnp.where(hits, gate_slots, 0.0).astype(BF16)


def down_kernel(active_ref, down_ref, out_ref):
    out_ref[...] = lax.dot_general(
        active_ref[...], down_ref[...], NT, preferred_element_type=F32
    ).astype(BF16)


def combine_kernel(back_ref, gate_ref, out_ref):
    out_ref[...] = lax.dot_general(
        back_ref[...], gate_ref[...], TN, preferred_element_type=F32
    )


def on_device(token_rows, row_scale, routes, gate_weights, up_weight, down_weight):
    experts = lax.axis_size("expert")
    shares = lax.axis_size("pipe")
    tokens, width = token_rows.shape
    hidden = up_weight.shape[2]
    capacity = tokens // 16
    slots = experts * capacity
    share_slots = slots // shares
    padded = -(-(width + 1) // 128) * 128
    params = pltpu.CompilerParams(vmem_limit_bytes=VMEM_LIMIT)
    rows_t = token_rows.T
    routes_t = routes.T
    gate_t = gate_weights.T
    scale_row = row_scale.reshape(1, tokens)

    send = pl.pallas_call(
        functools.partial(pick_kernel, experts, capacity),
        out_shape=jax.ShapeDtypeStruct((slots, padded), BF16),
        in_specs=[vmem_spec()] * 3,
        out_specs=vmem_spec(),
        compiler_params=params,
        name="pick",
    )(rows_t, scale_row, routes_t)
    got = lax.all_to_all(
        send.reshape(experts, capacity, padded), "expert", 0, 0, tiled=True
    ).reshape(slots, padded)
    gate_slots = pl.pallas_call(
        functools.partial(gate_kernel, experts, capacity),
        out_shape=jax.ShapeDtypeStruct((slots, tokens), BF16),
        in_specs=[vmem_spec()] * 2,
        out_specs=vmem_spec(),
        compiler_params=params,
        name="gates",
    )(routes_t, gate_t)

    terms = jnp.dot(got[:, :width], up_weight[0], preferred_element_type=F32)
    terms = (terms * WIRE_GAIN).astype(WIRE)
    parts = lax.all_to_all(
        terms.reshape(shares, share_slots, hidden), "pipe", 0, 0, tiled=True
    )
    share = lax.axis_index("pipe")
    mine = lax.dynamic_slice(got, (share * share_slots, width), (share_slots, 1))
    preact = jnp.sum(parts.astype(F32), axis=0) * (mine.astype(F32) * (1.0 / WIRE_GAIN))
    active = jax.nn.silu(preact).astype(BF16)
    active = jnp.broadcast_to(active[None], (shares, share_slots, hidden))
    active = lax.all_to_all(active, "pipe", 0, 0, tiled=True).reshape(slots, hidden)
    pieces = pl.pallas_call(
        down_kernel,
        grid=(4,),
        out_shape=jax.ShapeDtypeStruct((slots, width), BF16),
        in_specs=[
            pl.BlockSpec((slots // 4, hidden), lambda i: (i, 0)),
            pl.BlockSpec((width, hidden), lambda i: (0, 0)),
        ],
        out_specs=pl.BlockSpec((slots // 4, width), lambda i: (i, 0)),
        compiler_params=params,
        name="down",
    )(active, down_weight[0].T)
    back = lax.all_to_all(
        pieces.reshape(experts, capacity, width), "expert", 0, 0, tiled=True
    ).reshape(slots, width)
    combined_t = pl.pallas_call(
        combine_kernel,
        out_shape=jax.ShapeDtypeStruct((width, tokens), F32),
        in_specs=[vmem_spec()] * 2,
        out_specs=vmem_spec(),
        compiler_params=params,
        name="combine",
    )(back, gate_slots)
    return combined_t.T


def solution(mesh):
    return jax.shard_map(
        on_device,
        mesh=mesh,
        in_specs=(
            P("expert", "pipe"),
            P("expert"),
            P("expert", None),
            P("expert", None),
            P("expert", "pipe", None),
            P("expert", None, "pipe"),
        ),
        out_specs=P("expert", "pipe"),
        check_vma=False,
    )
```

```python
import functools
import math

import jax
import jax.numpy as jnp
from jax import lax
from jax.experimental import pallas as pl
from jax.experimental.pallas import tpu as pltpu
from jax.sharding import PartitionSpec as P

F32 = jnp.float32
BF16 = jnp.bfloat16
WIRE = jnp.float16
WIRE_GAIN = 16.0
ACTIVE_GAIN = 4.0
NT = (((1,), (1,)), ((), ()))
NN = (((1,), (0,)), ((), ()))
TN = (((0,), (0,)), ((), ()))
VMEM_LIMIT = 16 * 1024 * 1024


def vmem_spec():
    return pl.BlockSpec(memory_space=pltpu.VMEM)


def slot_hits(routes_t, experts, capacity):
    tokens = routes_t.shape[1]
    slots = experts * capacity
    expert_id = lax.broadcasted_iota(jnp.int32, (experts, tokens), 0)
    hot = jnp.zeros((experts, tokens), jnp.bool_)
    for k in range(routes_t.shape[0]):
        hot = hot | (routes_t[k : k + 1, :] == expert_id)
    hot_f = jnp.where(hot, 1.0, 0.0)
    before = lax.broadcasted_iota(jnp.int32, (tokens, tokens), 0) < lax.broadcasted_iota(
        jnp.int32, (tokens, tokens), 1
    )
    rank = lax.dot_general(
        hot_f.astype(BF16),
        jnp.where(before, 1.0, 0.0).astype(BF16),
        NN,
        preferred_element_type=F32,
    )
    rank = jnp.where(hot, rank, -1.0)
    rank_slots = jnp.broadcast_to(rank[:, None, :], (experts, capacity, tokens)).reshape(
        slots, tokens
    )
    place = (lax.broadcasted_iota(jnp.int32, (slots, tokens), 0) % capacity).astype(F32)
    return rank_slots == place


def pick_kernel(
    experts, capacity, rows_hbm, scale_hbm, routes_hbm, out_ref, rows_ref, scale_ref, routes_ref, sems
):
    copies = [
        pltpu.make_async_copy(src, dst, sems.at[i])
        for i, (src, dst) in enumerate(
            ((routes_hbm, routes_ref), (scale_hbm, scale_ref), (rows_hbm, rows_ref))
        )
    ]
    for copy in copies:
        copy.start()
    width = rows_ref.shape[0]
    copies[0].wait()
    hits = jnp.where(slot_hits(routes_ref[...], experts, capacity), 1.0, 0.0)
    copies[1].wait()
    scale = scale_ref[...].astype(F32).reshape(1, -1)
    scale = jnp.sum(hits * scale, axis=1, keepdims=True)
    copies[2].wait()
    picked = lax.dot_general(hits.astype(BF16), rows_ref[...], NT, preferred_element_type=F32)
    out_ref[:, :width] = picked.astype(BF16)
    out_ref[:, width:] = jnp.broadcast_to(
        scale.astype(BF16), (out_ref.shape[0], out_ref.shape[1] - width)
    )


def slot_gates(routes_t, gate_t, experts, capacity):
    tokens = routes_t.shape[1]
    expert_id = lax.broadcasted_iota(jnp.int32, (experts, tokens), 0)
    gate = jnp.zeros((experts, tokens), F32)
    for k in range(routes_t.shape[0]):
        gate = jnp.where(
            routes_t[k : k + 1, :] == expert_id, gate_t[k : k + 1, :].astype(F32), gate
        )
    gate_slots = jnp.broadcast_to(gate[:, None, :], (experts, capacity, tokens)).reshape(
        experts * capacity, tokens
    )
    hits = slot_hits(routes_t, experts, capacity)
    return jnp.where(hits, gate_slots, 0.0).astype(BF16)


def pack_kernel(capacity, rows_ref, out_ref):
    width = rows_ref.shape[1]
    whole = width // 128
    half = capacity // 2
    rest = width - whole * 128
    chunks = out_ref.shape[0]
    for j in range(whole):
        out_ref[:, j * capacity : (j + 1) * capacity, :] = rows_ref[
            :, j * 128 : (j + 1) * 128
        ].reshape(chunks, capacity, 128)
    tail = rows_ref[:, whole * 128 :].astype(F32).reshape(chunks, 2, half, rest)
    out_ref[:, whole * capacity :, :] = jnp.concatenate(
        [tail[:, 0], tail[:, 1]], axis=-1
    ).astype(BF16)


def combine_kernel(capacity, width, back_ref, routes_ref, gate_ref, out_ref):
    chunks = back_ref.shape[0]
    whole = width // 128
    half = capacity // 2
    rest = width - whole * 128
    gate = slot_gates(routes_ref[...], gate_ref[...], chunks, capacity)
    for j in range(whole):
        column = back_ref[:, j * capacity : (j + 1) * capacity, :].reshape(chunks * capacity, 128)
        out_ref[j * 128 : (j + 1) * 128, :] = lax.dot_general(
            column, gate, TN, preferred_element_type=F32
        )
    tail = back_ref[:, whole * capacity :, :].astype(F32)
    tail = jnp.stack([tail[:, :, :rest], tail[:, :, rest:]], axis=1)
    tail = tail.reshape(chunks * capacity, rest).astype(BF16)
    out_ref[whole * 128 :, :] = lax.dot_general(tail, gate, TN, preferred_element_type=F32)


def plane_groups(shares, experts, even_along_x):
    side = math.isqrt(shares)
    groups = []
    for expert in range(experts):
        along_x = (expert % 2 == 0) == even_along_x
        for line in range(side):
            shares_here = [line * side + i if along_x else i * side + line for i in range(side)]
            groups.append([share * experts + expert for share in shares_here])
    return groups


def on_device(token_rows, row_scale, routes, gate_weights, up_weight, down_weight):
    experts = lax.axis_size("expert")
    shares = lax.axis_size("pipe")
    tokens, width = token_rows.shape
    hidden = up_weight.shape[2]
    capacity = tokens // 16
    slots = experts * capacity
    padded = -(-(width + 1) // 128) * 128
    params = pltpu.CompilerParams(vmem_limit_bytes=VMEM_LIMIT)
    rows_t = token_rows.T
    routes_t = routes.T
    gate_t = gate_weights.T

    send = pl.pallas_call(
        functools.partial(pick_kernel, experts, capacity),
        out_shape=jax.ShapeDtypeStruct((slots, padded), BF16),
        in_specs=[pl.BlockSpec(memory_space=pltpu.HBM)] * 3,
        out_specs=vmem_spec(),
        scratch_shapes=[
            pltpu.VMEM((width, tokens), BF16),
            pltpu.VMEM((tokens,), BF16),
            pltpu.VMEM(routes_t.shape, jnp.int32),
            pltpu.SemaphoreType.DMA((3,)),
        ],
        name="pick",
    )(rows_t, row_scale, routes_t)
    got = lax.all_to_all(
        send.reshape(experts, capacity, padded), "expert", 0, 0, tiled=True
    ).reshape(slots, padded)
    scale = got[:, width : width + 1].astype(F32) * WIRE_GAIN
    terms = jnp.dot(got[:, :width], up_weight[0], preferred_element_type=F32)
    terms = (terms * scale).astype(WIRE)
    plane = ("pipe", "expert")
    first, second = plane_groups(shares, experts, True), plane_groups(shares, experts, False)
    side = len(first[0])
    side_slots = slots // side
    parts = lax.all_to_all(
        terms.reshape(side, side_slots, hidden), plane, 0, 0, tiled=True, axis_index_groups=first
    )
    partial = jnp.sum(parts.astype(F32), axis=0).astype(WIRE)
    partial = lax.all_gather(partial, plane, axis=0, axis_index_groups=second)
    preact = jnp.sum(partial.astype(F32), axis=0) * (1.0 / WIRE_GAIN)
    active = jax.nn.silu(preact).astype(BF16)
    active = (active.astype(F32) * ACTIVE_GAIN).astype(WIRE)
    active = lax.all_gather(active, plane, axis=0, tiled=True, axis_index_groups=first)
    active = (active.astype(F32) * (1.0 / ACTIVE_GAIN)).astype(BF16)
    pieces = jnp.dot(active, down_weight[0], preferred_element_type=F32).astype(BF16)
    pieces = pl.pallas_call(
        functools.partial(pack_kernel, capacity),
        out_shape=jax.ShapeDtypeStruct((experts, capacity * width // 128, 128), BF16),
        in_specs=[vmem_spec()],
        out_specs=vmem_spec(),
        compiler_params=params,
        name="pack",
    )(pieces)
    back = lax.all_to_all(pieces, "expert", 0, 0, tiled=True)
    combined_t = pl.pallas_call(
        functools.partial(combine_kernel, capacity, width),
        out_shape=jax.ShapeDtypeStruct((width, tokens), F32),
        in_specs=[vmem_spec()] * 3,
        out_specs=vmem_spec(),
        compiler_params=params,
        name="combine",
    )(back, routes_t, gate_t)
    return combined_t.T


def solution(mesh):
    return jax.shard_map(
        on_device,
        mesh=mesh,
        in_specs=(
            P("expert", "pipe"),
            P("expert"),
            P("expert", None),
            P("expert", None),
            P("expert", "pipe", None),
            P("expert", None, "pipe"),
        ),
        out_specs=P("expert", "pipe"),
        check_vma=False,
    )
```

```python
import functools
import math

import jax
import jax.numpy as jnp
from jax import lax
from jax.experimental import pallas as pl
from jax.experimental.pallas import tpu as pltpu
from jax.sharding import PartitionSpec as P

F32 = jnp.float32
BF16 = jnp.bfloat16
WIRE = jnp.float16
WIRE_GAIN = 16.0
ACTIVE_GAIN = 4.0
NT = (((1,), (1,)), ((), ()))
NN = (((1,), (0,)), ((), ()))
TN = (((0,), (0,)), ((), ()))
TILE = 512
VMEM_LIMIT = 24 * 1024 * 1024


def relabel(routes):
    return routes ^ (lax.axis_index("expert") % 2)


def vmem_spec():
    return pl.BlockSpec(memory_space=pltpu.VMEM)


def slot_hits(routes_t, experts, capacity):
    tokens = routes_t.shape[1]
    slots = experts * capacity
    expert_id = lax.broadcasted_iota(jnp.int32, (experts, tokens), 0)
    hot = jnp.zeros((experts, tokens), jnp.bool_)
    for k in range(routes_t.shape[0]):
        hot = hot | (routes_t[k : k + 1, :] == expert_id)
    hot_f = jnp.where(hot, 1.0, 0.0)
    before = lax.broadcasted_iota(jnp.int32, (tokens, tokens), 0) < lax.broadcasted_iota(
        jnp.int32, (tokens, tokens), 1
    )
    rank = lax.dot_general(
        hot_f.astype(BF16),
        jnp.where(before, 1.0, 0.0).astype(BF16),
        NN,
        preferred_element_type=F32,
    )
    rank = jnp.where(hot, rank, -1.0)
    rank_slots = jnp.broadcast_to(rank[:, None, :], (experts, capacity, tokens)).reshape(
        slots, tokens
    )
    place = (lax.broadcasted_iota(jnp.int32, (slots, tokens), 0) % capacity).astype(F32)
    return rank_slots == place


def pick_kernel(
    experts, capacity, rows_hbm, scale_hbm, routes_hbm, out_ref, rows_ref, scale_ref, routes_ref, sems
):
    copies = [
        pltpu.make_async_copy(src, dst, sems.at[i])
        for i, (src, dst) in enumerate(
            ((routes_hbm, routes_ref), (scale_hbm, scale_ref), (rows_hbm, rows_ref))
        )
    ]
    for copy in copies:
        copy.start()
    width = rows_ref.shape[0]
    copies[0].wait()
    hits = jnp.where(slot_hits(relabel(routes_ref[...]), experts, capacity), 1.0, 0.0)
    copies[1].wait()
    scale = scale_ref[...].astype(F32).reshape(1, -1)
    scale = jnp.sum(hits * scale, axis=1, keepdims=True)
    copies[2].wait()
    picked = lax.dot_general(hits.astype(BF16), rows_ref[...], NT, preferred_element_type=F32)
    out_ref[:, :width] = picked.astype(BF16)
    out_ref[:, width:] = jnp.broadcast_to(
        scale.astype(BF16), (out_ref.shape[0], out_ref.shape[1] - width)
    )


def slot_gates(routes_t, gate_t, experts, capacity):
    tokens = routes_t.shape[1]
    expert_id = lax.broadcasted_iota(jnp.int32, (experts, tokens), 0)
    gate = jnp.zeros((experts, tokens), F32)
    for k in range(routes_t.shape[0]):
        gate = jnp.where(
            routes_t[k : k + 1, :] == expert_id, gate_t[k : k + 1, :].astype(F32), gate
        )
    gate_slots = jnp.broadcast_to(gate[:, None, :], (experts, capacity, tokens)).reshape(
        experts * capacity, tokens
    )
    hits = slot_hits(routes_t, experts, capacity)
    return jnp.where(hits, gate_slots, 0.0).astype(BF16)


def pair_kernel(own_ref, other_ref, later_ref, out_ref, mark_ref):
    out_ref[0] = own_ref[...]
    out_ref[1] = other_ref[...]
    mark_ref[...] = jnp.zeros(mark_ref.shape, F32)


def join_kernel(got_ref, mark_ref, out_ref):
    out_ref[...] = mark_ref[...]


def up_kernel(capacity, got_ref, weight_ref, out_ref):
    width, hidden = weight_ref.shape[1:]
    slots = got_ref.shape[0] * capacity
    for i in range(2):
        rows = got_ref[:, i * capacity : (i + 1) * capacity, :].reshape(slots, got_ref.shape[2])
        scale = rows[:, width : width + 1].astype(F32) * WIRE_GAIN
        rows = rows[:, :width]
        for j in range(0, hidden, TILE):
            term = jnp.dot(rows, weight_ref[i, :, j : j + TILE], preferred_element_type=F32)
            out_ref[i * slots : (i + 1) * slots, j : j + TILE] = term * scale


def down_kernel(capacity, own_ref, active_ref, weight_ref, out_ref):
    width = weight_ref.shape[0]
    whole = width // 128
    half = capacity // 2
    rest = width - whole * 128
    chunks = out_ref.shape[0]
    other = lax.dot_general(active_ref[...], weight_ref[...], NT, preferred_element_type=F32)
    for i, piece in enumerate((own_ref[...].astype(F32), other)):
        for j in range(whole):
            out_ref[:, i, j * capacity : (j + 1) * capacity, :] = (
                piece[:, j * 128 : (j + 1) * 128].astype(BF16).reshape(chunks, capacity, 128)
            )
        tail = piece[:, whole * 128 :].reshape(chunks, 2, half, rest)
        out_ref[:, i, whole * capacity :, :] = jnp.concatenate(
            [tail[:, 0], tail[:, 1]], axis=-1
        ).astype(BF16)


def combine_kernel(capacity, width, back_ref, routes_ref, gate_ref, out_ref):
    chunks = back_ref.shape[0]
    whole = width // 128
    half = capacity // 2
    rest = width - whole * 128
    gate = slot_gates(relabel(routes_ref[...]), gate_ref[...], chunks, capacity)
    for j in range(whole):
        column = back_ref[:, j * capacity : (j + 1) * capacity, :].reshape(chunks * capacity, 128)
        out_ref[j * 128 : (j + 1) * 128, :] = lax.dot_general(
            column, gate, TN, preferred_element_type=F32
        )
    tail = back_ref[:, whole * capacity :, :].astype(F32)
    tail = jnp.stack([tail[:, :, :rest], tail[:, :, rest:]], axis=1)
    tail = tail.reshape(chunks * capacity, rest).astype(BF16)
    out_ref[whole * 128 :, :] = lax.dot_general(tail, gate, TN, preferred_element_type=F32)


def plane_groups(shares, experts, even_along_x):
    side = math.isqrt(shares)
    groups = []
    for expert in range(experts):
        along_x = (expert % 2 == 0) == even_along_x
        for line in range(side):
            shares_here = [line * side + i if along_x else i * side + line for i in range(side)]
            groups.append([share * experts + expert for share in shares_here])
    return groups


def on_device(token_rows, row_scale, routes, gate_weights, up_weight, down_weight):
    experts = lax.axis_size("expert")
    shares = lax.axis_size("pipe")
    tokens, width = token_rows.shape
    hidden = up_weight.shape[2]
    capacity = tokens // 16
    slots = experts * capacity
    padded = -(-(width + 1) // 128) * 128
    params = pltpu.CompilerParams(vmem_limit_bytes=VMEM_LIMIT)
    rows_t = token_rows.T
    routes_t = routes.T
    gate_t = gate_weights.T

    send = pl.pallas_call(
        functools.partial(pick_kernel, experts, capacity),
        out_shape=jax.ShapeDtypeStruct((slots, padded), BF16),
        in_specs=[pl.BlockSpec(memory_space=pltpu.HBM)] * 3,
        out_specs=vmem_spec(),
        scratch_shapes=[
            pltpu.VMEM((width, tokens), BF16),
            pltpu.VMEM((tokens,), BF16),
            pltpu.VMEM(routes_t.shape, jnp.int32),
            pltpu.SemaphoreType.DMA((3,)),
        ],
        name="pick",
    )(rows_t, row_scale, routes_t)
    chips = experts // 2
    rings = [[2 * chip + core for chip in range(chips)] for core in range(2)]
    swap = [(i, i ^ 1) for i in range(experts)]
    up_own, down_own = up_weight[0], down_weight[0].T
    up_other = lax.ppermute(up_own, "expert", swap)
    down_other = lax.ppermute(down_own, "expert", swap)
    got = lax.all_to_all(
        send.reshape(chips, 2 * capacity, padded), "expert", 0, 0, tiled=True,
        axis_index_groups=rings,
    )
    anywhere = pl.BlockSpec(memory_space=pl.ANY)
    up_both, mark = pl.pallas_call(
        pair_kernel,
        out_shape=[
            jax.ShapeDtypeStruct((2, width, hidden), BF16),
            jax.ShapeDtypeStruct((8, hidden), F32),
        ],
        in_specs=[vmem_spec(), vmem_spec(), anywhere],
        out_specs=[vmem_spec()] * 2,
        compiler_params=params,
        cost_estimate=pl.CostEstimate(flops=0, bytes_accessed=100000, transcendentals=0),
        name="pair",
    )(up_own, up_other, down_other)
    after = pl.pallas_call(
        join_kernel,
        out_shape=jax.ShapeDtypeStruct((8, hidden), F32),
        in_specs=[anywhere, vmem_spec()],
        out_specs=vmem_spec(),
        compiler_params=params,
        name="join",
    )(got, mark)
    after = lax.ppermute(after, "expert", swap)
    terms = pl.pallas_call(
        functools.partial(up_kernel, capacity),
        out_shape=jax.ShapeDtypeStruct((slots, hidden), F32),
        in_specs=[vmem_spec()] * 2,
        out_specs=vmem_spec(),
        compiler_params=params,
        name="up",
    )(got, up_both)
    terms = (terms + after[:1]).astype(WIRE)
    plane = ("pipe", "expert")
    first, second = plane_groups(shares, experts, True), plane_groups(shares, experts, False)
    side = len(first[0])
    side_slots = slots // side
    parts = lax.all_to_all(
        terms.reshape(side, side_slots, hidden), plane, 0, 0, tiled=True, axis_index_groups=first
    )
    partial = jnp.sum(parts.astype(F32), axis=0).astype(WIRE)
    partial = lax.all_gather(partial, plane, axis=0, axis_index_groups=second)
    preact = jnp.sum(partial.astype(F32), axis=0) * (1.0 / WIRE_GAIN)
    active = jax.nn.silu(preact).astype(BF16)
    active = (active.astype(F32) * ACTIVE_GAIN).astype(WIRE)
    active = lax.all_gather(active, plane, axis=0, tiled=True, axis_index_groups=first)
    own, other = (
        (rows.astype(F32) * (1.0 / ACTIVE_GAIN)).astype(BF16) for rows in jnp.split(active, 2)
    )
    own = lax.dot_general(own, down_own, NT, preferred_element_type=F32).astype(BF16)
    packed = capacity * width // 128
    pieces = pl.pallas_call(
        functools.partial(down_kernel, capacity),
        out_shape=jax.ShapeDtypeStruct((chips, 2, packed, 128), BF16),
        in_specs=[vmem_spec()] * 3,
        out_specs=vmem_spec(),
        compiler_params=params,
        name="down",
    )(own, other, down_other)
    back = lax.all_to_all(
        pieces.reshape(chips, 2 * packed, 128), "expert", 0, 0, tiled=True, axis_index_groups=rings
    ).reshape(experts, packed, 128)
    combined_t = pl.pallas_call(
        functools.partial(combine_kernel, capacity, width),
        out_shape=jax.ShapeDtypeStruct((width, tokens), F32),
        in_specs=[vmem_spec()] * 3,
        out_specs=vmem_spec(),
        compiler_params=params,
        name="combine",
    )(back, routes_t, gate_t)
    return combined_t.T


def solution(mesh):
    return jax.shard_map(
        on_device,
        mesh=mesh,
        in_specs=(
            P("expert", "pipe"),
            P("expert"),
            P("expert", None),
            P("expert", None),
            P("expert", "pipe", None),
            P("expert", None, "pipe"),
        ),
        out_specs=P("expert", "pipe"),
        check_vma=False,
    )
```

```python
import functools
import math

import jax
import jax.numpy as jnp
from jax import lax
from jax.experimental import pallas as pl
from jax.experimental.pallas import tpu as pltpu
from jax.sharding import PartitionSpec as P

F32 = jnp.float32
BF16 = jnp.bfloat16
WIRE = jnp.float16
WIRE_GAIN = 16.0
ACTIVE_GAIN = 4.0
NT = (((1,), (1,)), ((), ()))
NN = (((1,), (0,)), ((), ()))
TN = (((0,), (0,)), ((), ()))
TILE = 512
VMEM_LIMIT = 24 * 1024 * 1024


def relabel(routes):
    return routes ^ (lax.axis_index("expert") % 2)


def vmem_spec():
    return pl.BlockSpec(memory_space=pltpu.VMEM)


def slot_hits(routes_t, experts, capacity):
    tokens = routes_t.shape[1]
    slots = experts * capacity
    expert_id = lax.broadcasted_iota(jnp.int32, (experts, tokens), 0)
    hot = jnp.zeros((experts, tokens), jnp.bool_)
    for k in range(routes_t.shape[0]):
        hot = hot | (routes_t[k : k + 1, :] == expert_id)
    hot_f = jnp.where(hot, 1.0, 0.0)
    before = lax.broadcasted_iota(jnp.int32, (tokens, tokens), 0) < lax.broadcasted_iota(
        jnp.int32, (tokens, tokens), 1
    )
    rank = lax.dot_general(
        hot_f.astype(BF16),
        jnp.where(before, 1.0, 0.0).astype(BF16),
        NN,
        preferred_element_type=F32,
    )
    rank = jnp.where(hot, rank, -1.0)
    rank_slots = jnp.broadcast_to(rank[:, None, :], (experts, capacity, tokens)).reshape(
        slots, tokens
    )
    place = (lax.broadcasted_iota(jnp.int32, (slots, tokens), 0) % capacity).astype(F32)
    return rank_slots == place


def pick_kernel(
    experts, capacity, rows_hbm, scale_hbm, routes_hbm, out_ref, rows_ref, scale_ref, routes_ref, sems
):
    copies = [
        pltpu.make_async_copy(src, dst, sems.at[i])
        for i, (src, dst) in enumerate(
            ((routes_hbm, routes_ref), (scale_hbm, scale_ref), (rows_hbm, rows_ref))
        )
    ]
    for copy in copies:
        copy.start()
    width = rows_ref.shape[0]
    copies[0].wait()
    hits = jnp.where(slot_hits(relabel(routes_ref[...]), experts, capacity), 1.0, 0.0)
    copies[1].wait()
    scale = scale_ref[...].astype(F32).reshape(1, -1)
    scale = jnp.sum(hits * scale, axis=1, keepdims=True)
    copies[2].wait()
    picked = lax.dot_general(hits.astype(BF16), rows_ref[...], NT, preferred_element_type=F32)
    out_ref[:, :width] = picked.astype(BF16)
    out_ref[:, width:] = jnp.broadcast_to(
        scale.astype(BF16), (out_ref.shape[0], out_ref.shape[1] - width)
    )


def slot_gates(routes_t, gate_t, experts, capacity):
    tokens = routes_t.shape[1]
    expert_id = lax.broadcasted_iota(jnp.int32, (experts, tokens), 0)
    gate = jnp.zeros((experts, tokens), F32)
    for k in range(routes_t.shape[0]):
        gate = jnp.where(
            routes_t[k : k + 1, :] == expert_id, gate_t[k : k + 1, :].astype(F32), gate
        )
    gate_slots = jnp.broadcast_to(gate[:, None, :], (experts, capacity, tokens)).reshape(
        experts * capacity, tokens
    )
    hits = slot_hits(routes_t, experts, capacity)
    return jnp.where(hits, gate_slots, 0.0).astype(BF16)


def join_kernel(got_ref, later_ref, out_ref):
    out_ref[...] = jnp.zeros(out_ref.shape, F32)


def up_kernel(capacity, got_ref, own_ref, other_hbm, out_ref, other_ref, sem):
    copy = pltpu.make_async_copy(other_hbm, other_ref, sem)
    copy.start()
    width, hidden = own_ref.shape
    slots = got_ref.shape[0] * capacity
    for i, weight_ref in enumerate((own_ref, other_ref)):
        if i == 1:
            copy.wait()
        rows = got_ref[:, i * capacity : (i + 1) * capacity, :].reshape(slots, got_ref.shape[2])
        scale = rows[:, width : width + 1].astype(F32) * WIRE_GAIN
        rows = rows[:, :width]
        for j in range(0, hidden, TILE):
            term = jnp.dot(rows, weight_ref[:, j : j + TILE], preferred_element_type=F32)
            out_ref[i * slots : (i + 1) * slots, j : j + TILE] = term * scale


def down_kernel(capacity, own_ref, active_ref, weight_ref, out_ref):
    width = weight_ref.shape[0]
    whole = width // 128
    half = capacity // 2
    rest = width - whole * 128
    chunks = out_ref.shape[0]
    other = lax.dot_general(active_ref[...], weight_ref[...], NT, preferred_element_type=F32)
    for i, piece in enumerate((own_ref[...].astype(F32), other)):
        for j in range(whole):
            out_ref[:, i, j * capacity : (j + 1) * capacity, :] = (
                piece[:, j * 128 : (j + 1) * 128].astype(BF16).reshape(chunks, capacity, 128)
            )
        tail = piece[:, whole * 128 :].reshape(chunks, 2, half, rest)
        out_ref[:, i, whole * capacity :, :] = jnp.concatenate(
            [tail[:, 0], tail[:, 1]], axis=-1
        ).astype(BF16)


def combine_kernel(capacity, width, back_ref, routes_ref, gate_ref, out_ref):
    chunks = back_ref.shape[0]
    whole = width // 128
    half = capacity // 2
    rest = width - whole * 128
    gate = slot_gates(relabel(routes_ref[...]), gate_ref[...], chunks, capacity)
    for j in range(whole):
        column = back_ref[:, j * capacity : (j + 1) * capacity, :].reshape(chunks * capacity, 128)
        out_ref[j * 128 : (j + 1) * 128, :] = lax.dot_general(
            column, gate, TN, preferred_element_type=F32
        )
    tail = back_ref[:, whole * capacity :, :].astype(F32)
    tail = jnp.stack([tail[:, :, :rest], tail[:, :, rest:]], axis=1)
    tail = tail.reshape(chunks * capacity, rest).astype(BF16)
    out_ref[whole * 128 :, :] = lax.dot_general(tail, gate, TN, preferred_element_type=F32)


def plane_groups(shares, experts, even_along_x):
    side = math.isqrt(shares)
    groups = []
    for expert in range(experts):
        along_x = (expert % 2 == 0) == even_along_x
        for line in range(side):
            shares_here = [line * side + i if along_x else i * side + line for i in range(side)]
            groups.append([share * experts + expert for share in shares_here])
    return groups


def on_device(token_rows, row_scale, routes, gate_weights, up_weight, down_weight):
    experts = lax.axis_size("expert")
    shares = lax.axis_size("pipe")
    tokens, width = token_rows.shape
    hidden = up_weight.shape[2]
    capacity = tokens // 16
    slots = experts * capacity
    padded = -(-(width + 1) // 128) * 128
    params = pltpu.CompilerParams(vmem_limit_bytes=VMEM_LIMIT)
    rows_t = token_rows.T
    routes_t = routes.T
    gate_t = gate_weights.T

    send = pl.pallas_call(
        functools.partial(pick_kernel, experts, capacity),
        out_shape=jax.ShapeDtypeStruct((slots, padded), BF16),
        in_specs=[pl.BlockSpec(memory_space=pltpu.HBM)] * 3,
        out_specs=vmem_spec(),
        scratch_shapes=[
            pltpu.VMEM((width, tokens), BF16),
            pltpu.VMEM((tokens,), BF16),
            pltpu.VMEM(routes_t.shape, jnp.int32),
            pltpu.SemaphoreType.DMA((3,)),
        ],
        name="pick",
    )(rows_t, row_scale, routes_t)
    chips = experts // 2
    rings = [[2 * chip + core for chip in range(chips)] for core in range(2)]
    swap = [(i, i ^ 1) for i in range(experts)]
    up_own, down_own = up_weight[0], down_weight[0].T
    up_other = lax.ppermute(up_own, "expert", swap)
    down_other = lax.ppermute(down_own, "expert", swap)
    got = lax.all_to_all(
        send.reshape(chips, 2 * capacity, padded), "expert", 0, 0, tiled=True,
        axis_index_groups=rings,
    )
    anywhere = pl.BlockSpec(memory_space=pl.ANY)
    after = pl.pallas_call(
        join_kernel,
        out_shape=jax.ShapeDtypeStruct((8, hidden), F32),
        in_specs=[anywhere] * 2,
        out_specs=vmem_spec(),
        compiler_params=params,
        name="join",
    )(got, down_other)
    after = lax.ppermute(after, "expert", swap)
    terms = pl.pallas_call(
        functools.partial(up_kernel, capacity),
        out_shape=jax.ShapeDtypeStruct((slots, hidden), F32),
        in_specs=[vmem_spec(), vmem_spec(), anywhere],
        out_specs=vmem_spec(),
        scratch_shapes=[pltpu.VMEM((width, hidden), BF16), pltpu.SemaphoreType.DMA],
        compiler_params=params,
        name="up",
    )(got, up_own, up_other)
    terms = (terms + after[:1]).astype(WIRE)
    plane = ("pipe", "expert")
    first, second = plane_groups(shares, experts, True), plane_groups(shares, experts, False)
    side = len(first[0])
    side_slots = slots // side
    parts = lax.all_to_all(
        terms.reshape(side, side_slots, hidden), plane, 0, 0, tiled=True, axis_index_groups=first
    )
    partial = sum(parts[i].astype(F32) for i in range(side)).astype(WIRE)
    partial = lax.all_gather(partial, plane, axis=0, axis_index_groups=second)
    preact = sum(partial[i].astype(F32) for i in range(side)) * (1.0 / WIRE_GAIN)
    active = jax.nn.silu(preact).astype(BF16)
    active = (active.astype(F32) * ACTIVE_GAIN).astype(WIRE)
    active = lax.all_gather(active, plane, axis=0, tiled=True, axis_index_groups=first)
    own, other = (
        (rows.astype(F32) * (1.0 / ACTIVE_GAIN)).astype(BF16) for rows in jnp.split(active, 2)
    )
    own = lax.dot_general(own, down_own, NT, preferred_element_type=F32).astype(BF16)
    packed = capacity * width // 128
    pieces = pl.pallas_call(
        functools.partial(down_kernel, capacity),
        out_shape=jax.ShapeDtypeStruct((chips, 2, packed, 128), BF16),
        in_specs=[vmem_spec()] * 3,
        out_specs=vmem_spec(),
        compiler_params=params,
        name="down",
    )(own, other, down_other)
    back = lax.all_to_all(
        pieces.reshape(chips, 2 * packed, 128), "expert", 0, 0, tiled=True, axis_index_groups=rings
    ).reshape(experts, packed, 128)
    combined_t = pl.pallas_call(
        functools.partial(combine_kernel, capacity, width),
        out_shape=jax.ShapeDtypeStruct((width, tokens), F32),
        in_specs=[vmem_spec()] * 3,
        out_specs=vmem_spec(),
        compiler_params=params,
        name="combine",
    )(back, routes_t, gate_t)
    return combined_t.T


def solution(mesh):
    return jax.shard_map(
        on_device,
        mesh=mesh,
        in_specs=(
            P("expert", "pipe"),
            P("expert"),
            P("expert", None),
            P("expert", None),
            P("expert", "pipe", None),
            P("expert", None, "pipe"),
        ),
        out_specs=P("expert", "pipe"),
        check_vma=False,
    )
```

```python
import functools
import math

import jax
import jax.numpy as jnp
from jax import lax
from jax.experimental import pallas as pl
from jax.experimental.pallas import tpu as pltpu
from jax.sharding import PartitionSpec as P

F32 = jnp.float32
BF16 = jnp.bfloat16
WIRE = jnp.float16
WIRE_GAIN = 16.0
ACTIVE_GAIN = 4.0
NT = (((1,), (1,)), ((), ()))
NN = (((1,), (0,)), ((), ()))
TN = (((0,), (0,)), ((), ()))
TILE = 512
VMEM_LIMIT = 24 * 1024 * 1024


def relabel(routes):
    return routes ^ (lax.axis_index("expert") % 2)


def vmem_spec():
    return pl.BlockSpec(memory_space=pltpu.VMEM)


def slot_hits(routes_t, experts, capacity):
    tokens = routes_t.shape[1]
    slots = experts * capacity
    expert_id = lax.broadcasted_iota(jnp.int32, (experts, tokens), 0)
    hot = jnp.zeros((experts, tokens), jnp.bool_)
    for k in range(routes_t.shape[0]):
        hot = hot | (routes_t[k : k + 1, :] == expert_id)
    hot_f = jnp.where(hot, 1.0, 0.0)
    before = lax.broadcasted_iota(jnp.int32, (tokens, tokens), 0) < lax.broadcasted_iota(
        jnp.int32, (tokens, tokens), 1
    )
    rank = lax.dot_general(
        hot_f.astype(BF16),
        jnp.where(before, 1.0, 0.0).astype(BF16),
        NN,
        preferred_element_type=F32,
    )
    rank = jnp.where(hot, rank, -1.0)
    rank_slots = jnp.broadcast_to(rank[:, None, :], (experts, capacity, tokens)).reshape(
        slots, tokens
    )
    place = (lax.broadcasted_iota(jnp.int32, (slots, tokens), 0) % capacity).astype(F32)
    return rank_slots == place


def pick_kernel(
    experts, capacity, rows_hbm, scale_hbm, routes_hbm, out_ref, rows_ref, scale_ref, routes_ref, sems
):
    copies = [
        pltpu.make_async_copy(src, dst, sems.at[i])
        for i, (src, dst) in enumerate(
            ((routes_hbm, routes_ref), (scale_hbm, scale_ref), (rows_hbm, rows_ref))
        )
    ]
    for copy in copies:
        copy.start()
    copies[0].wait()
    hits = jnp.where(slot_hits(relabel(routes_ref[...]), experts, capacity), 1.0, 0.0)
    copies[1].wait()
    scale = scale_ref[...].astype(F32).reshape(1, -1)
    scale = jnp.sum(hits * scale, axis=1, keepdims=True)
    copies[2].wait()
    picked = lax.dot_general(hits.astype(BF16), rows_ref[...], NT, preferred_element_type=F32)
    width = rows_ref.shape[0]
    whole = width // 128
    half = capacity // 2
    chunks = out_ref.shape[0]
    picked = picked.reshape(chunks, 2, capacity, width)
    tails = picked[..., whole * 128 :].reshape(chunks, 2, 2, half, width - whole * 128)
    for i in range(2):
        for j in range(whole):
            at = (i * whole + j) * capacity
            out_ref[:, at : at + capacity, :] = picked[:, i, :, j * 128 : (j + 1) * 128].astype(BF16)
        at = 2 * whole * capacity + i * half
        out_ref[:, at : at + half, :] = jnp.concatenate(
            [tails[:, i, 0], tails[:, i, 1]], axis=-1
        ).astype(BF16)
    scale = jnp.broadcast_to(scale, (scale.shape[0], 32)).reshape(chunks, 4, half, 32)
    out_ref[:, 2 * capacity * width // 128 :, :] = jnp.concatenate(
        [scale[:, g] for g in range(4)], axis=-1
    ).astype(BF16)


def slot_gates(routes_t, gate_t, experts, capacity):
    tokens = routes_t.shape[1]
    expert_id = lax.broadcasted_iota(jnp.int32, (experts, tokens), 0)
    gate = jnp.zeros((experts, tokens), F32)
    for k in range(routes_t.shape[0]):
        gate = jnp.where(
            routes_t[k : k + 1, :] == expert_id, gate_t[k : k + 1, :].astype(F32), gate
        )
    gate_slots = jnp.broadcast_to(gate[:, None, :], (experts, capacity, tokens)).reshape(
        experts * capacity, tokens
    )
    hits = slot_hits(routes_t, experts, capacity)
    return jnp.where(hits, gate_slots, 0.0).astype(BF16)


def join_kernel(got_ref, later_ref, out_ref):
    out_ref[...] = jnp.zeros(out_ref.shape, F32)


def up_kernel(capacity, got_ref, own_ref, other_hbm, out_ref, other_ref, sem):
    copy = pltpu.make_async_copy(other_hbm, other_ref, sem)
    copy.start()
    width, hidden = own_ref.shape
    chunks = got_ref.shape[0]
    slots = chunks * capacity
    whole = width // 128
    half = capacity // 2
    rest = width - whole * 128
    scales = got_ref[:, 2 * capacity * width // 128 :, :].astype(F32)
    for i, weight_ref in enumerate((own_ref, other_ref)):
        if i == 1:
            copy.wait()
        columns = []
        for j in range(whole):
            at = (i * whole + j) * capacity
            columns.append(got_ref[:, at : at + capacity, :].reshape(slots, 128))
        at = 2 * whole * capacity + i * half
        tail = got_ref[:, at : at + half, :].astype(F32)
        tail = jnp.stack([tail[:, :, :rest], tail[:, :, rest:]], axis=1)
        columns.append(tail.reshape(slots, rest).astype(BF16))
        rows = jnp.concatenate(columns, axis=1)
        scale = jnp.stack([scales[:, :, 64 * i : 64 * i + 1], scales[:, :, 64 * i + 32 : 64 * i + 33]], axis=1)
        scale = scale.reshape(slots, 1) * WIRE_GAIN
        for j in range(0, hidden, TILE):
            term = jnp.dot(rows, weight_ref[:, j : j + TILE], preferred_element_type=F32)
            out_ref[i * slots : (i + 1) * slots, j : j + TILE] = term * scale


def down_kernel(capacity, own_ref, active_ref, weight_ref, out_ref):
    width = weight_ref.shape[0]
    whole = width // 128
    half = capacity // 2
    rest = width - whole * 128
    chunks = out_ref.shape[0]
    other = lax.dot_general(active_ref[...], weight_ref[...], NT, preferred_element_type=F32)
    for i, piece in enumerate((own_ref[...].astype(F32), other)):
        for j in range(whole):
            out_ref[:, i, j * capacity : (j + 1) * capacity, :] = (
                piece[:, j * 128 : (j + 1) * 128].astype(BF16).reshape(chunks, capacity, 128)
            )
        tail = piece[:, whole * 128 :].reshape(chunks, 2, half, rest)
        out_ref[:, i, whole * capacity :, :] = jnp.concatenate(
            [tail[:, 0], tail[:, 1]], axis=-1
        ).astype(BF16)


def combine_kernel(capacity, width, back_ref, routes_ref, gate_ref, out_ref):
    chunks = back_ref.shape[0]
    whole = width // 128
    half = capacity // 2
    rest = width - whole * 128
    gate = slot_gates(relabel(routes_ref[...]), gate_ref[...], chunks, capacity)
    for j in range(whole):
        column = back_ref[:, j * capacity : (j + 1) * capacity, :].reshape(chunks * capacity, 128)
        out_ref[j * 128 : (j + 1) * 128, :] = lax.dot_general(
            column, gate, TN, preferred_element_type=F32
        )
    tail = back_ref[:, whole * capacity :, :].astype(F32)
    tail = jnp.stack([tail[:, :, :rest], tail[:, :, rest:]], axis=1)
    tail = tail.reshape(chunks * capacity, rest).astype(BF16)
    out_ref[whole * 128 :, :] = lax.dot_general(tail, gate, TN, preferred_element_type=F32)


def plane_groups(shares, experts, even_along_x):
    side = math.isqrt(shares)
    groups = []
    for expert in range(experts):
        along_x = (expert % 2 == 0) == even_along_x
        for line in range(side):
            shares_here = [line * side + i if along_x else i * side + line for i in range(side)]
            groups.append([share * experts + expert for share in shares_here])
    return groups


def on_device(token_rows, row_scale, routes, gate_weights, up_weight, down_weight):
    experts = lax.axis_size("expert")
    shares = lax.axis_size("pipe")
    tokens, width = token_rows.shape
    hidden = up_weight.shape[2]
    capacity = tokens // 16
    slots = experts * capacity
    chips = experts // 2
    sent = 2 * capacity * width // 128 + capacity // 2
    params = pltpu.CompilerParams(vmem_limit_bytes=VMEM_LIMIT)
    rows_t = token_rows.T
    routes_t = routes.T
    gate_t = gate_weights.T

    send = pl.pallas_call(
        functools.partial(pick_kernel, experts, capacity),
        out_shape=jax.ShapeDtypeStruct((chips, sent, 128), BF16),
        in_specs=[pl.BlockSpec(memory_space=pltpu.HBM)] * 3,
        out_specs=vmem_spec(),
        scratch_shapes=[
            pltpu.VMEM((width, tokens), BF16),
            pltpu.VMEM((tokens,), BF16),
            pltpu.VMEM(routes_t.shape, jnp.int32),
            pltpu.SemaphoreType.DMA((3,)),
        ],
        name="pick",
    )(rows_t, row_scale, routes_t)
    rings = [[2 * chip + core for chip in range(chips)] for core in range(2)]
    swap = [(i, i ^ 1) for i in range(experts)]
    up_own, down_own = up_weight[0], down_weight[0].T
    up_other = lax.ppermute(up_own, "expert", swap)
    down_other = lax.ppermute(down_own, "expert", swap)
    got = lax.all_to_all(
        send, "expert", 0, 0, tiled=True, axis_index_groups=rings
    )
    anywhere = pl.BlockSpec(memory_space=pl.ANY)
    after = pl.pallas_call(
        join_kernel,
        out_shape=jax.ShapeDtypeStruct((8, hidden), F32),
        in_specs=[anywhere] * 2,
        out_specs=vmem_spec(),
        compiler_params=params,
        name="join",
    )(got, down_other)
    after = lax.ppermute(after, "expert", swap)
    terms = pl.pallas_call(
        functools.partial(up_kernel, capacity),
        out_shape=jax.ShapeDtypeStruct((slots, hidden), F32),
        in_specs=[vmem_spec(), vmem_spec(), anywhere],
        out_specs=vmem_spec(),
        scratch_shapes=[pltpu.VMEM((width, hidden), BF16), pltpu.SemaphoreType.DMA],
        compiler_params=params,
        name="up",
    )(got, up_own, up_other)
    terms = (terms + after[:1]).astype(WIRE)
    plane = ("pipe", "expert")
    first, second = plane_groups(shares, experts, True), plane_groups(shares, experts, False)
    side = len(first[0])
    side_slots = slots // side
    parts = lax.all_to_all(
        terms.reshape(side, side_slots, hidden), plane, 0, 0, tiled=True, axis_index_groups=first
    )
    partial = sum(parts[i].astype(F32) for i in range(side)).astype(WIRE)
    partial = lax.all_gather(partial, plane, axis=0, axis_index_groups=second)
    preact = sum(partial[i].astype(F32) for i in range(side)) * (1.0 / WIRE_GAIN)
    active = jax.nn.silu(preact).astype(BF16)
    active = (active.astype(F32) * ACTIVE_GAIN).astype(WIRE)
    active = lax.all_gather(active, plane, axis=0, tiled=True, axis_index_groups=first)
    own, other = (
        (rows.astype(F32) * (1.0 / ACTIVE_GAIN)).astype(BF16) for rows in jnp.split(active, 2)
    )
    own = lax.dot_general(own, down_own, NT, preferred_element_type=F32).astype(BF16)
    packed = capacity * width // 128
    pieces = pl.pallas_call(
        functools.partial(down_kernel, capacity),
        out_shape=jax.ShapeDtypeStruct((chips, 2, packed, 128), BF16),
        in_specs=[vmem_spec()] * 3,
        out_specs=vmem_spec(),
        compiler_params=params,
        name="down",
    )(own, other, down_other)
    back = lax.all_to_all(
        pieces.reshape(chips, 2 * packed, 128), "expert", 0, 0, tiled=True, axis_index_groups=rings
    ).reshape(experts, packed, 128)
    combined_t = pl.pallas_call(
        functools.partial(combine_kernel, capacity, width),
        out_shape=jax.ShapeDtypeStruct((width, tokens), F32),
        in_specs=[vmem_spec()] * 3,
        out_specs=vmem_spec(),
        compiler_params=params,
        name="combine",
    )(back, routes_t, gate_t)
    return combined_t.T


def solution(mesh):
    return jax.shard_map(
        on_device,
        mesh=mesh,
        in_specs=(
            P("expert", "pipe"),
            P("expert"),
            P("expert", None),
            P("expert", None),
            P("expert", "pipe", None),
            P("expert", None, "pipe"),
        ),
        out_specs=P("expert", "pipe"),
        check_vma=False,
    )
```

```python
import functools
import math

import jax
import jax.numpy as jnp
from jax import lax
from jax.experimental import pallas as pl
from jax.experimental.pallas import tpu as pltpu
from jax.sharding import PartitionSpec as P

F32 = jnp.float32
BF16 = jnp.bfloat16
WIRE = jnp.float16
WIRE_GAIN = 16.0
ACTIVE_GAIN = 4.0
NT = (((1,), (1,)), ((), ()))
NN = (((1,), (0,)), ((), ()))
TN = (((0,), (0,)), ((), ()))
TILE = 512
VMEM_LIMIT = 24 * 1024 * 1024


def relabel(routes):
    return routes ^ (lax.axis_index("expert") % 2)


def vmem_spec():
    return pl.BlockSpec(memory_space=pltpu.VMEM)


def slot_hits(routes_t, experts, capacity):
    tokens = routes_t.shape[1]
    slots = experts * capacity
    expert_id = lax.broadcasted_iota(jnp.int32, (experts, tokens), 0)
    hot = jnp.zeros((experts, tokens), jnp.bool_)
    for k in range(routes_t.shape[0]):
        hot = hot | (routes_t[k : k + 1, :] == expert_id)
    hot_f = jnp.where(hot, 1.0, 0.0)
    before = lax.broadcasted_iota(jnp.int32, (tokens, tokens), 0) < lax.broadcasted_iota(
        jnp.int32, (tokens, tokens), 1
    )
    rank = lax.dot_general(
        hot_f.astype(BF16),
        jnp.where(before, 1.0, 0.0).astype(BF16),
        NN,
        preferred_element_type=F32,
    )
    rank = jnp.where(hot, rank, -1.0)
    rank_slots = jnp.broadcast_to(rank[:, None, :], (experts, capacity, tokens)).reshape(
        slots, tokens
    )
    place = (lax.broadcasted_iota(jnp.int32, (slots, tokens), 0) % capacity).astype(F32)
    return rank_slots == place


def pick_kernel(
    experts, capacity, rows_hbm, scale_hbm, routes_hbm, out_ref, rows_ref, scale_ref, routes_ref, sems
):
    copies = [
        pltpu.make_async_copy(src, dst, sems.at[i])
        for i, (src, dst) in enumerate(
            ((routes_hbm, routes_ref), (scale_hbm, scale_ref), (rows_hbm, rows_ref))
        )
    ]
    for copy in copies:
        copy.start()
    copies[0].wait()
    hits = jnp.where(slot_hits(relabel(routes_ref[...]), experts, capacity), 1.0, 0.0)
    copies[1].wait()
    scale = scale_ref[...].astype(F32).reshape(1, -1)
    scale = jnp.sum(hits * scale, axis=1, keepdims=True)
    copies[2].wait()
    picked = lax.dot_general(hits.astype(BF16), rows_ref[...], NT, preferred_element_type=F32)
    width = rows_ref.shape[0]
    whole = width // 128
    half = capacity // 2
    chunks = out_ref.shape[0]
    picked = picked.reshape(chunks, 2, capacity, width)
    tails = picked[..., whole * 128 :].reshape(chunks, 2, 2, half, width - whole * 128)
    for i in range(2):
        for j in range(whole):
            at = (i * whole + j) * capacity
            out_ref[:, at : at + capacity, :] = picked[:, i, :, j * 128 : (j + 1) * 128].astype(BF16)
        at = 2 * whole * capacity + i * half
        out_ref[:, at : at + half, :] = jnp.concatenate(
            [tails[:, i, 0], tails[:, i, 1]], axis=-1
        ).astype(BF16)
    scale = jnp.broadcast_to(scale, (scale.shape[0], 32)).reshape(chunks, 4, half, 32)
    out_ref[:, 2 * capacity * width // 128 :, :] = jnp.concatenate(
        [scale[:, g] for g in range(4)], axis=-1
    ).astype(BF16)


def slot_gates(routes_t, gate_t, experts, capacity):
    tokens = routes_t.shape[1]
    expert_id = lax.broadcasted_iota(jnp.int32, (experts, tokens), 0)
    gate = jnp.zeros((experts, tokens), F32)
    for k in range(routes_t.shape[0]):
        gate = jnp.where(
            routes_t[k : k + 1, :] == expert_id, gate_t[k : k + 1, :].astype(F32), gate
        )
    gate_slots = jnp.broadcast_to(gate[:, None, :], (experts, capacity, tokens)).reshape(
        experts * capacity, tokens
    )
    hits = slot_hits(routes_t, experts, capacity)
    return jnp.where(hits, gate_slots, 0.0).astype(BF16)


def join_kernel(got_ref, later_ref, out_ref):
    out_ref[...] = jnp.zeros(out_ref.shape, F32)


def up_kernel(capacity, got_ref, own_ref, other_hbm, out_ref, other_ref, sem):
    copy = pltpu.make_async_copy(other_hbm, other_ref, sem)
    copy.start()
    width, hidden = own_ref.shape
    chunks = got_ref.shape[0]
    slots = chunks * capacity
    whole = width // 128
    half = capacity // 2
    rest = width - whole * 128
    scales = got_ref[:, 2 * capacity * width // 128 :, :].astype(F32)
    for i, weight_ref in enumerate((own_ref, other_ref)):
        if i == 1:
            copy.wait()
        columns = []
        for j in range(whole):
            at = (i * whole + j) * capacity
            columns.append(got_ref[:, at : at + capacity, :].reshape(slots, 128))
        at = 2 * whole * capacity + i * half
        tail = got_ref[:, at : at + half, :].astype(F32)
        tail = jnp.stack([tail[:, :, :rest], tail[:, :, rest:]], axis=1)
        columns.append(tail.reshape(slots, rest).astype(BF16))
        rows = jnp.concatenate(columns, axis=1)
        scale = jnp.stack([scales[:, :, 64 * i : 64 * i + 1], scales[:, :, 64 * i + 32 : 64 * i + 33]], axis=1)
        scale = scale.reshape(slots, 1) * WIRE_GAIN
        for j in range(0, hidden, TILE):
            term = jnp.dot(rows, weight_ref[:, j : j + TILE], preferred_element_type=F32)
            out_ref[i * slots : (i + 1) * slots, j : j + TILE] = term * scale


def down_kernel(capacity, own_ref, active_ref, weight_ref, out_ref):
    width = weight_ref.shape[0]
    whole = width // 128
    half = capacity // 2
    rest = width - whole * 128
    chunks = out_ref.shape[0]
    other = lax.dot_general(active_ref[...], weight_ref[...], NT, preferred_element_type=F32)
    for i, piece in enumerate((own_ref[...].astype(F32), other)):
        for j in range(whole):
            out_ref[:, i, j * capacity : (j + 1) * capacity, :] = (
                piece[:, j * 128 : (j + 1) * 128].astype(BF16).reshape(chunks, capacity, 128)
            )
        tail = piece[:, whole * 128 :].reshape(chunks, 2, half, rest)
        out_ref[:, i, whole * capacity :, :] = jnp.concatenate(
            [tail[:, 0], tail[:, 1]], axis=-1
        ).astype(BF16)


def combine_kernel(capacity, width, back_ref, routes_ref, gate_ref, out_ref):
    chunks = back_ref.shape[0]
    whole = width // 128
    half = capacity // 2
    rest = width - whole * 128
    gate = slot_gates(relabel(routes_ref[...]), gate_ref[...], chunks, capacity)
    for j in range(whole):
        column = back_ref[:, j * capacity : (j + 1) * capacity, :].reshape(chunks * capacity, 128)
        out_ref[j * 128 : (j + 1) * 128, :] = lax.dot_general(
            column, gate, TN, preferred_element_type=F32
        )
    tail = back_ref[:, whole * capacity :, :].astype(F32)
    tail = jnp.stack([tail[:, :, :rest], tail[:, :, rest:]], axis=1)
    tail = tail.reshape(chunks * capacity, rest).astype(BF16)
    out_ref[whole * 128 :, :] = lax.dot_general(tail, gate, TN, preferred_element_type=F32)


def plane_groups(shares, experts, even_along_x):
    side = math.isqrt(shares)
    groups = []
    for expert in range(experts):
        along_x = (expert % 2 == 0) == even_along_x
        for line in range(side):
            shares_here = [line * side + i if along_x else i * side + line for i in range(side)]
            groups.append([share * experts + expert for share in shares_here])
    return groups


def on_device(token_rows, row_scale, routes, gate_weights, up_weight, down_weight):
    experts = lax.axis_size("expert")
    shares = lax.axis_size("pipe")
    tokens, width = token_rows.shape
    hidden = up_weight.shape[2]
    capacity = tokens // 16
    slots = experts * capacity
    chips = experts // 2
    sent = 2 * capacity * width // 128 + capacity // 2
    params = pltpu.CompilerParams(vmem_limit_bytes=VMEM_LIMIT)
    rows_t = token_rows.T
    routes_t = routes.T
    gate_t = gate_weights.T

    send = pl.pallas_call(
        functools.partial(pick_kernel, experts, capacity),
        out_shape=jax.ShapeDtypeStruct((chips, sent, 128), BF16),
        in_specs=[pl.BlockSpec(memory_space=pltpu.HBM)] * 3,
        out_specs=vmem_spec(),
        scratch_shapes=[
            pltpu.VMEM((width, tokens), BF16),
            pltpu.VMEM((tokens,), BF16),
            pltpu.VMEM(routes_t.shape, jnp.int32),
            pltpu.SemaphoreType.DMA((3,)),
        ],
        name="pick",
    )(rows_t, row_scale, routes_t)
    rings = [[2 * chip + core for chip in range(chips)] for core in range(2)]
    swap = [(i, i ^ 1) for i in range(experts)]
    up_own, down_own = up_weight[0], down_weight[0].T
    up_other = lax.ppermute(up_own, "expert", swap)
    down_other = lax.ppermute(down_own, "expert", swap)
    got = lax.all_to_all(
        send, "expert", 0, 0, tiled=True, axis_index_groups=rings
    )
    anywhere = pl.BlockSpec(memory_space=pl.ANY)
    after = pl.pallas_call(
        join_kernel,
        out_shape=jax.ShapeDtypeStruct((8, hidden), F32),
        in_specs=[anywhere] * 2,
        out_specs=vmem_spec(),
        compiler_params=params,
        name="join",
    )(got, down_other)
    after = lax.ppermute(after, "expert", [(i, i + 1) for i in range(0, experts, 2)])
    terms = pl.pallas_call(
        functools.partial(up_kernel, capacity),
        out_shape=jax.ShapeDtypeStruct((slots, hidden), F32),
        in_specs=[vmem_spec(), vmem_spec(), anywhere],
        out_specs=vmem_spec(),
        scratch_shapes=[pltpu.VMEM((width, hidden), BF16), pltpu.SemaphoreType.DMA],
        compiler_params=params,
        name="up",
    )(got, up_own, up_other)
    terms = (terms + after[:1]).astype(WIRE)
    plane = ("pipe", "expert")
    first, second = plane_groups(shares, experts, False), plane_groups(shares, experts, True)
    side = len(first[0])
    side_slots = slots // side
    parts = lax.all_to_all(
        terms.reshape(side, side_slots, hidden), plane, 0, 0, tiled=True, axis_index_groups=first
    )
    partial = sum(parts[i].astype(F32) for i in range(side)).astype(WIRE)
    partial = lax.all_gather(partial, plane, axis=0, axis_index_groups=second)
    preact = sum(partial[i].astype(F32) for i in range(side)) * (1.0 / WIRE_GAIN)
    active = jax.nn.silu(preact).astype(BF16)
    active = (active.astype(F32) * ACTIVE_GAIN).astype(WIRE)
    active = lax.all_gather(active, plane, axis=0, tiled=True, axis_index_groups=first)
    own, other = (
        (rows.astype(F32) * (1.0 / ACTIVE_GAIN)).astype(BF16) for rows in jnp.split(active, 2)
    )
    own = lax.dot_general(own, down_own, NT, preferred_element_type=F32).astype(BF16)
    packed = capacity * width // 128
    pieces = pl.pallas_call(
        functools.partial(down_kernel, capacity),
        out_shape=jax.ShapeDtypeStruct((chips, 2, packed, 128), BF16),
        in_specs=[vmem_spec()] * 3,
        out_specs=vmem_spec(),
        compiler_params=params,
        name="down",
    )(own, other, down_other)
    back = lax.all_to_all(
        pieces.reshape(chips, 2 * packed, 128), "expert", 0, 0, tiled=True, axis_index_groups=rings
    ).reshape(experts, packed, 128)
    combined_t = pl.pallas_call(
        functools.partial(combine_kernel, capacity, width),
        out_shape=jax.ShapeDtypeStruct((width, tokens), F32),
        in_specs=[vmem_spec()] * 3,
        out_specs=vmem_spec(),
        compiler_params=params,
        name="combine",
    )(back, routes_t, gate_t)
    return combined_t.T


def solution(mesh):
    return jax.shard_map(
        on_device,
        mesh=mesh,
        in_specs=(
            P("expert", "pipe"),
            P("expert"),
            P("expert", None),
            P("expert", None),
            P("expert", "pipe", None),
            P("expert", None, "pipe"),
        ),
        out_specs=P("expert", "pipe"),
        check_vma=False,
    )
```

```python
import functools
import math

import jax
import jax.numpy as jnp
from jax import lax
from jax.experimental import pallas as pl
from jax.experimental.pallas import tpu as pltpu
from jax.sharding import PartitionSpec as P

F32 = jnp.float32
BF16 = jnp.bfloat16
WIRE = jnp.float16
WIRE_GAIN = 16.0
ACTIVE_GAIN = 4.0
NT = (((1,), (1,)), ((), ()))
NN = (((1,), (0,)), ((), ()))
TN = (((0,), (0,)), ((), ()))
TILE = 512
VMEM_LIMIT = 24 * 1024 * 1024


def relabel(routes):
    return routes ^ (lax.axis_index("expert") % 2)


def vmem_spec():
    return pl.BlockSpec(memory_space=pltpu.VMEM)


def slot_hits(routes_t, experts, capacity):
    tokens = routes_t.shape[1]
    slots = experts * capacity
    expert_id = lax.broadcasted_iota(jnp.int32, (experts, tokens), 0)
    hot = jnp.zeros((experts, tokens), jnp.bool_)
    for k in range(routes_t.shape[0]):
        hot = hot | (routes_t[k : k + 1, :] == expert_id)
    hot_f = jnp.where(hot, 1.0, 0.0)
    before = lax.broadcasted_iota(jnp.int32, (tokens, tokens), 0) < lax.broadcasted_iota(
        jnp.int32, (tokens, tokens), 1
    )
    rank = lax.dot_general(
        hot_f.astype(BF16),
        jnp.where(before, 1.0, 0.0).astype(BF16),
        NN,
        preferred_element_type=F32,
    )
    rank = jnp.where(hot, rank, -1.0)
    rank_slots = jnp.broadcast_to(rank[:, None, :], (experts, capacity, tokens)).reshape(
        slots, tokens
    )
    place = (lax.broadcasted_iota(jnp.int32, (slots, tokens), 0) % capacity).astype(F32)
    return rank_slots == place


def pick_kernel(
    experts, capacity, rows_hbm, scale_hbm, routes_hbm, out_ref, rows_ref, scale_ref, routes_ref, sems
):
    copies = [
        pltpu.make_async_copy(src, dst, sems.at[i])
        for i, (src, dst) in enumerate(
            ((routes_hbm, routes_ref), (scale_hbm, scale_ref), (rows_hbm, rows_ref))
        )
    ]
    for copy in copies:
        copy.start()
    copies[0].wait()
    hits = jnp.where(slot_hits(relabel(routes_ref[...]), experts, capacity), 1.0, 0.0)
    copies[1].wait()
    scale = scale_ref[...].astype(F32).reshape(1, -1)
    scale = jnp.sum(hits * scale, axis=1, keepdims=True)
    copies[2].wait()
    picked = lax.dot_general(hits.astype(BF16), rows_ref[...], NT, preferred_element_type=F32)
    width = rows_ref.shape[0]
    whole = width // 128
    half = capacity // 2
    chunks = out_ref.shape[0]
    picked = picked.reshape(chunks, 2, capacity, width)
    tails = picked[..., whole * 128 :].reshape(chunks, 2, 2, half, width - whole * 128)
    for i in range(2):
        for j in range(whole):
            at = (i * whole + j) * capacity
            out_ref[:, at : at + capacity, :] = picked[:, i, :, j * 128 : (j + 1) * 128].astype(BF16)
    tails = jnp.concatenate([tails[:, :, 0], tails[:, :, 1]], axis=-1)
    at = 2 * whole * capacity
    out_ref[:, at : at + capacity, :] = tails.reshape(chunks, capacity, 128).astype(BF16)
    scale = jnp.broadcast_to(scale, (scale.shape[0], 32)).reshape(chunks, 4, half, 32)
    out_ref[:, 2 * capacity * width // 128 :, :] = jnp.concatenate(
        [scale[:, g] for g in range(4)], axis=-1
    ).astype(BF16)


def slot_gates(routes_t, gate_t, experts, capacity):
    tokens = routes_t.shape[1]
    expert_id = lax.broadcasted_iota(jnp.int32, (experts, tokens), 0)
    gate = jnp.zeros((experts, tokens), F32)
    for k in range(routes_t.shape[0]):
        gate = jnp.where(
            routes_t[k : k + 1, :] == expert_id, gate_t[k : k + 1, :].astype(F32), gate
        )
    gate_slots = jnp.broadcast_to(gate[:, None, :], (experts, capacity, tokens)).reshape(
        experts * capacity, tokens
    )
    hits = slot_hits(routes_t, experts, capacity)
    return jnp.where(hits, gate_slots, 0.0).astype(BF16)


def join_kernel(got_ref, later_ref, out_ref):
    out_ref[...] = jnp.zeros(out_ref.shape, F32)


def up_kernel(capacity, got_ref, own_ref, other_hbm, out_ref, other_ref, sem):
    copy = pltpu.make_async_copy(other_hbm, other_ref, sem)
    copy.start()
    width, hidden = own_ref.shape
    chunks = got_ref.shape[0]
    slots = chunks * capacity
    whole = width // 128
    half = capacity // 2
    rest = width - whole * 128
    at = 2 * whole * capacity
    tails = got_ref[:, at : at + capacity, :].astype(F32)
    scales = got_ref[:, at + capacity :, :].astype(F32)
    for i, weight_ref in enumerate((own_ref, other_ref)):
        if i == 1:
            copy.wait()
        columns = []
        for j in range(whole):
            at = (i * whole + j) * capacity
            columns.append(got_ref[:, at : at + capacity, :].reshape(slots, 128))
        tail = tails[:, i * half : (i + 1) * half, :]
        tail = jnp.stack([tail[:, :, :rest], tail[:, :, rest:]], axis=1)
        columns.append(tail.reshape(slots, rest).astype(BF16))
        rows = jnp.concatenate(columns, axis=1)
        scale = jnp.stack([scales[:, :, 64 * i : 64 * i + 1], scales[:, :, 64 * i + 32 : 64 * i + 33]], axis=1)
        scale = scale.reshape(slots, 1) * WIRE_GAIN
        for j in range(0, hidden, TILE):
            term = jnp.dot(rows, weight_ref[:, j : j + TILE], preferred_element_type=F32)
            out_ref[i * slots : (i + 1) * slots, j : j + TILE] = term * scale


def down_kernel(capacity, own_ref, active_ref, weight_ref, out_ref):
    width = weight_ref.shape[0]
    whole = width // 128
    half = capacity // 2
    rest = width - whole * 128
    chunks = out_ref.shape[0]
    other = lax.dot_general(active_ref[...], weight_ref[...], NT, preferred_element_type=F32)
    tails = []
    for i, piece in enumerate((own_ref[...].astype(F32), other)):
        for j in range(whole):
            at = (i * whole + j) * capacity
            out_ref[:, at : at + capacity, :] = (
                piece[:, j * 128 : (j + 1) * 128].astype(BF16).reshape(chunks, capacity, 128)
            )
        tail = piece[:, whole * 128 :].reshape(chunks, 2, half, rest)
        tails.append(jnp.concatenate([tail[:, 0], tail[:, 1]], axis=-1))
    out_ref[:, 2 * whole * capacity :, :] = jnp.concatenate(tails, axis=1).astype(BF16)


def combine_kernel(capacity, width, back_ref, routes_ref, gate_ref, out_ref):
    chunks = back_ref.shape[0]
    whole = width // 128
    half = capacity // 2
    rest = width - whole * 128
    slots = chunks * 2 * capacity
    gate = slot_gates(relabel(routes_ref[...]), gate_ref[...], chunks * 2, capacity)
    for j in range(whole):
        column = jnp.stack(
            [
                back_ref[:, at : at + capacity, :]
                for at in (j * capacity, (whole + j) * capacity)
            ],
            axis=1,
        )
        out_ref[j * 128 : (j + 1) * 128, :] = lax.dot_general(
            column.reshape(slots, 128), gate, TN, preferred_element_type=F32
        )
    tails = back_ref[:, 2 * whole * capacity :, :].astype(F32).reshape(chunks, 2, half, 128)
    tails = jnp.stack([tails[..., :rest], tails[..., rest:]], axis=2)
    tails = tails.reshape(slots, rest).astype(BF16)
    out_ref[whole * 128 :, :] = lax.dot_general(tails, gate, TN, preferred_element_type=F32)


def plane_groups(shares, experts, even_along_x):
    side = math.isqrt(shares)
    groups = []
    for expert in range(experts):
        along_x = (expert % 2 == 0) == even_along_x
        for line in range(side):
            shares_here = [line * side + i if along_x else i * side + line for i in range(side)]
            groups.append([share * experts + expert for share in shares_here])
    return groups


def on_device(token_rows, row_scale, routes, gate_weights, up_weight, down_weight):
    experts = lax.axis_size("expert")
    shares = lax.axis_size("pipe")
    tokens, width = token_rows.shape
    hidden = up_weight.shape[2]
    capacity = tokens // 16
    slots = experts * capacity
    chips = experts // 2
    sent = 2 * capacity * width // 128 + capacity // 2
    params = pltpu.CompilerParams(vmem_limit_bytes=VMEM_LIMIT)
    rows_t = token_rows.T
    routes_t = routes.T
    gate_t = gate_weights.T

    send = pl.pallas_call(
        functools.partial(pick_kernel, experts, capacity),
        out_shape=jax.ShapeDtypeStruct((chips, sent, 128), BF16),
        in_specs=[pl.BlockSpec(memory_space=pltpu.HBM)] * 3,
        out_specs=vmem_spec(),
        scratch_shapes=[
            pltpu.VMEM((width, tokens), BF16),
            pltpu.VMEM((tokens,), BF16),
            pltpu.VMEM(routes_t.shape, jnp.int32),
            pltpu.SemaphoreType.DMA((3,)),
        ],
        name="pick",
    )(rows_t, row_scale, routes_t)
    rings = [[2 * chip + core for chip in range(chips)] for core in range(2)]
    swap = [(i, i ^ 1) for i in range(experts)]
    up_own, down_own = up_weight[0], down_weight[0].T
    up_other = lax.ppermute(up_own, "expert", swap)
    down_other = lax.ppermute(down_own, "expert", swap)
    got = lax.all_to_all(
        send, "expert", 0, 0, tiled=True, axis_index_groups=rings
    )
    anywhere = pl.BlockSpec(memory_space=pl.ANY)
    after = pl.pallas_call(
        join_kernel,
        out_shape=jax.ShapeDtypeStruct((8, hidden), F32),
        in_specs=[anywhere] * 2,
        out_specs=vmem_spec(),
        compiler_params=params,
        name="join",
    )(got, down_other)
    after = lax.ppermute(after, "expert", [(i, i + 1) for i in range(0, experts, 2)])
    terms = pl.pallas_call(
        functools.partial(up_kernel, capacity),
        out_shape=jax.ShapeDtypeStruct((slots, hidden), F32),
        in_specs=[vmem_spec(), vmem_spec(), anywhere],
        out_specs=vmem_spec(),
        scratch_shapes=[pltpu.VMEM((width, hidden), BF16), pltpu.SemaphoreType.DMA],
        compiler_params=params,
        name="up",
    )(got, up_own, up_other)
    terms = (terms + after[:1]).astype(WIRE)
    plane = ("pipe", "expert")
    first, second = plane_groups(shares, experts, False), plane_groups(shares, experts, True)
    side = len(first[0])
    side_slots = slots // side
    parts = lax.all_to_all(
        terms.reshape(side, side_slots, hidden), plane, 0, 0, tiled=True, axis_index_groups=first
    )
    partial = sum(parts[i].astype(F32) for i in range(side)).astype(WIRE)
    partial = lax.all_gather(partial, plane, axis=0, axis_index_groups=second)
    preact = sum(partial[i].astype(F32) for i in range(side)) * (1.0 / WIRE_GAIN)
    active = jax.nn.silu(preact).astype(BF16)
    active = (active.astype(F32) * ACTIVE_GAIN).astype(WIRE)
    active = lax.all_gather(active, plane, axis=0, tiled=True, axis_index_groups=first)
    own, other = (
        (rows.astype(F32) * (1.0 / ACTIVE_GAIN)).astype(BF16) for rows in jnp.split(active, 2)
    )
    own = lax.dot_general(own, down_own, NT, preferred_element_type=F32).astype(BF16)
    pieces = pl.pallas_call(
        functools.partial(down_kernel, capacity),
        out_shape=jax.ShapeDtypeStruct((chips, 2 * capacity * width // 128, 128), BF16),
        in_specs=[vmem_spec()] * 3,
        out_specs=vmem_spec(),
        compiler_params=params,
        name="down",
    )(own, other, down_other)
    back = lax.all_to_all(pieces, "expert", 0, 0, tiled=True, axis_index_groups=rings)
    combined_t = pl.pallas_call(
        functools.partial(combine_kernel, capacity, width),
        out_shape=jax.ShapeDtypeStruct((width, tokens), F32),
        in_specs=[vmem_spec()] * 3,
        out_specs=vmem_spec(),
        compiler_params=params,
        name="combine",
    )(back, routes_t, gate_t)
    return combined_t.T


def solution(mesh):
    return jax.shard_map(
        on_device,
        mesh=mesh,
        in_specs=(
            P("expert", "pipe"),
            P("expert"),
            P("expert", None),
            P("expert", None),
            P("expert", "pipe", None),
            P("expert", None, "pipe"),
        ),
        out_specs=P("expert", "pipe"),
        check_vma=False,
    )
```

```python
import functools
import math

import jax
import jax.numpy as jnp
from jax import lax
from jax.experimental import pallas as pl
from jax.experimental.pallas import tpu as pltpu
from jax.sharding import PartitionSpec as P

F32 = jnp.float32
BF16 = jnp.bfloat16
WIRE = jnp.float16
WIRE_GAIN = 16.0
ACTIVE_GAIN = 4.0
NT = (((1,), (1,)), ((), ()))
NN = (((1,), (0,)), ((), ()))
TN = (((0,), (0,)), ((), ()))
TILE = 512
VMEM_LIMIT = 24 * 1024 * 1024


def relabel(routes):
    return routes ^ (lax.axis_index("expert") % 2)


def vmem_spec():
    return pl.BlockSpec(memory_space=pltpu.VMEM)


def slot_hits(routes_t, experts, capacity):
    tokens = routes_t.shape[1]
    slots = experts * capacity
    expert_id = lax.broadcasted_iota(jnp.int32, (experts, tokens), 0)
    hot = jnp.zeros((experts, tokens), jnp.bool_)
    for k in range(routes_t.shape[0]):
        hot = hot | (routes_t[k : k + 1, :] == expert_id)
    hot_f = jnp.where(hot, 1.0, 0.0)
    before = lax.broadcasted_iota(jnp.int32, (tokens, tokens), 0) < lax.broadcasted_iota(
        jnp.int32, (tokens, tokens), 1
    )
    rank = lax.dot_general(
        hot_f.astype(BF16),
        jnp.where(before, 1.0, 0.0).astype(BF16),
        NN,
        preferred_element_type=F32,
    )
    rank = jnp.where(hot, rank, -1.0)
    rank_slots = jnp.broadcast_to(rank[:, None, :], (experts, capacity, tokens)).reshape(
        slots, tokens
    )
    place = (lax.broadcasted_iota(jnp.int32, (slots, tokens), 0) % capacity).astype(F32)
    return rank_slots == place


def pick_kernel(
    experts, capacity, rows_hbm, scale_hbm, routes_hbm, out_ref, rows_ref, scale_ref, routes_ref, sems
):
    copies = [
        pltpu.make_async_copy(src, dst, sems.at[i])
        for i, (src, dst) in enumerate(
            ((routes_hbm, routes_ref), (scale_hbm, scale_ref), (rows_hbm, rows_ref))
        )
    ]
    for copy in copies:
        copy.start()
    copies[0].wait()
    hits = jnp.where(slot_hits(relabel(routes_ref[...]), experts, capacity), 1.0, 0.0)
    copies[1].wait()
    scale = scale_ref[...].astype(F32).reshape(1, -1)
    scale = jnp.sum(hits * scale, axis=1, keepdims=True)
    copies[2].wait()
    picked = lax.dot_general(hits.astype(BF16), rows_ref[...], NT, preferred_element_type=F32)
    width = rows_ref.shape[0]
    whole = width // 128
    half = capacity // 2
    chunks = out_ref.shape[0]
    picked = picked.reshape(chunks, 2, capacity, width)
    tails = picked[..., whole * 128 :].reshape(chunks, 2, 2, half, width - whole * 128)
    for i in range(2):
        for j in range(whole):
            at = (i * whole + j) * capacity
            out_ref[:, at : at + capacity, :] = picked[:, i, :, j * 128 : (j + 1) * 128].astype(BF16)
    tails = jnp.concatenate([tails[:, :, 0], tails[:, :, 1]], axis=-1)
    at = 2 * whole * capacity
    out_ref[:, at : at + capacity, :] = tails.reshape(chunks, capacity, 128).astype(BF16)
    scale = jnp.broadcast_to(scale, (scale.shape[0], 32)).reshape(chunks, 4, half, 32)
    out_ref[:, 2 * capacity * width // 128 :, :] = jnp.concatenate(
        [scale[:, g] for g in range(4)], axis=-1
    ).astype(BF16)


def slot_gates(routes_t, gate_t, experts, capacity):
    tokens = routes_t.shape[1]
    expert_id = lax.broadcasted_iota(jnp.int32, (experts, tokens), 0)
    gate = jnp.zeros((experts, tokens), F32)
    for k in range(routes_t.shape[0]):
        gate = jnp.where(
            routes_t[k : k + 1, :] == expert_id, gate_t[k : k + 1, :].astype(F32), gate
        )
    gate_slots = jnp.broadcast_to(gate[:, None, :], (experts, capacity, tokens)).reshape(
        experts * capacity, tokens
    )
    hits = slot_hits(routes_t, experts, capacity)
    return jnp.where(hits, gate_slots, 0.0).astype(BF16)


def join_kernel(got_ref, later_ref, out_ref):
    out_ref[...] = jnp.zeros(out_ref.shape, F32)


def up_kernel(capacity, got_ref, own_ref, other_hbm, out_ref, other_ref, sem):
    copy = pltpu.make_async_copy(other_hbm, other_ref, sem)
    copy.start()
    width, hidden = own_ref.shape
    chunks = got_ref.shape[0]
    slots = chunks * capacity
    whole = width // 128
    half = capacity // 2
    rest = width - whole * 128
    at = 2 * whole * capacity
    tails = got_ref[:, at : at + capacity, :].astype(F32)
    scales = got_ref[:, at + capacity :, :].astype(F32)
    for i, weight_ref in enumerate((own_ref, other_ref)):
        if i == 1:
            copy.wait()
        columns = []
        for j in range(whole):
            at = (i * whole + j) * capacity
            columns.append(got_ref[:, at : at + capacity, :].reshape(slots, 128))
        tail = tails[:, i * half : (i + 1) * half, :]
        tail = jnp.stack([tail[:, :, :rest], tail[:, :, rest:]], axis=1)
        columns.append(tail.reshape(slots, rest).astype(BF16))
        rows = jnp.concatenate(columns, axis=1)
        scale = jnp.stack([scales[:, :, 64 * i : 64 * i + 1], scales[:, :, 64 * i + 32 : 64 * i + 33]], axis=1)
        scale = scale.reshape(slots, 1) * WIRE_GAIN
        for j in range(0, hidden, TILE):
            term = jnp.dot(rows, weight_ref[:, j : j + TILE], preferred_element_type=F32)
            out_ref[i * slots : (i + 1) * slots, j : j + TILE] = term * scale


def pack_kernel(capacity, own_ref, other_ref, out_ref):
    width = own_ref.shape[1]
    whole = width // 128
    half = capacity // 2
    rest = width - whole * 128
    chunks = out_ref.shape[0]
    tails = []
    for i, piece in enumerate((own_ref[...].astype(F32), other_ref[...].astype(F32))):
        for j in range(whole):
            at = (i * whole + j) * capacity
            out_ref[:, at : at + capacity, :] = (
                piece[:, j * 128 : (j + 1) * 128].astype(BF16).reshape(chunks, capacity, 128)
            )
        tail = piece[:, whole * 128 :].reshape(chunks, 2, half, rest)
        tails.append(jnp.concatenate([tail[:, 0], tail[:, 1]], axis=-1))
    out_ref[:, 2 * whole * capacity :, :] = jnp.concatenate(tails, axis=1).astype(BF16)


def combine_kernel(capacity, width, back_ref, routes_ref, gate_ref, out_ref):
    chunks = back_ref.shape[0]
    whole = width // 128
    half = capacity // 2
    rest = width - whole * 128
    slots = chunks * 2 * capacity
    gate = slot_gates(relabel(routes_ref[...]), gate_ref[...], chunks * 2, capacity)
    for j in range(whole):
        column = jnp.stack(
            [
                back_ref[:, at : at + capacity, :]
                for at in (j * capacity, (whole + j) * capacity)
            ],
            axis=1,
        )
        out_ref[j * 128 : (j + 1) * 128, :] = lax.dot_general(
            column.reshape(slots, 128), gate, TN, preferred_element_type=F32
        )
    tails = back_ref[:, 2 * whole * capacity :, :].astype(F32).reshape(chunks, 2, half, 128)
    tails = jnp.stack([tails[..., :rest], tails[..., rest:]], axis=2)
    tails = tails.reshape(slots, rest).astype(BF16)
    out_ref[whole * 128 :, :] = lax.dot_general(tails, gate, TN, preferred_element_type=F32)


def plane_groups(shares, experts, even_along_x):
    side = math.isqrt(shares)
    groups = []
    for expert in range(experts):
        along_x = (expert % 2 == 0) == even_along_x
        for line in range(side):
            shares_here = [line * side + i if along_x else i * side + line for i in range(side)]
            groups.append([share * experts + expert for share in shares_here])
    return groups


def on_device(token_rows, row_scale, routes, gate_weights, up_weight, down_weight):
    experts = lax.axis_size("expert")
    shares = lax.axis_size("pipe")
    tokens, width = token_rows.shape
    hidden = up_weight.shape[2]
    capacity = tokens // 16
    slots = experts * capacity
    chips = experts // 2
    sent = 2 * capacity * width // 128 + capacity // 2
    params = pltpu.CompilerParams(vmem_limit_bytes=VMEM_LIMIT)
    rows_t = token_rows.T
    routes_t = routes.T
    gate_t = gate_weights.T

    send = pl.pallas_call(
        functools.partial(pick_kernel, experts, capacity),
        out_shape=jax.ShapeDtypeStruct((chips, sent, 128), BF16),
        in_specs=[pl.BlockSpec(memory_space=pltpu.HBM)] * 3,
        out_specs=vmem_spec(),
        scratch_shapes=[
            pltpu.VMEM((width, tokens), BF16),
            pltpu.VMEM((tokens,), BF16),
            pltpu.VMEM(routes_t.shape, jnp.int32),
            pltpu.SemaphoreType.DMA((3,)),
        ],
        name="pick",
    )(rows_t, row_scale, routes_t)
    rings = [[2 * chip + core for chip in range(chips)] for core in range(2)]
    swap = [(i, i ^ 1) for i in range(experts)]
    up_own, down_own = up_weight[0], down_weight[0].T
    up_other = lax.ppermute(up_own, "expert", swap)
    down_other = lax.ppermute(down_own, "expert", swap)
    got = lax.all_to_all(
        send, "expert", 0, 0, tiled=True, axis_index_groups=rings
    )
    anywhere = pl.BlockSpec(memory_space=pl.ANY)
    after = pl.pallas_call(
        join_kernel,
        out_shape=jax.ShapeDtypeStruct((8, hidden), F32),
        in_specs=[anywhere] * 2,
        out_specs=vmem_spec(),
        compiler_params=params,
        name="join",
    )(got, down_other)
    after = lax.ppermute(after, "expert", [(i, i + 1) for i in range(0, experts, 2)])
    terms = pl.pallas_call(
        functools.partial(up_kernel, capacity),
        out_shape=jax.ShapeDtypeStruct((slots, hidden), F32),
        in_specs=[vmem_spec(), vmem_spec(), anywhere],
        out_specs=vmem_spec(),
        scratch_shapes=[pltpu.VMEM((width, hidden), BF16), pltpu.SemaphoreType.DMA],
        compiler_params=params,
        name="up",
    )(got, up_own, up_other)
    terms = (terms + after[:1]).astype(WIRE)
    plane = ("pipe", "expert")
    first, second = plane_groups(shares, experts, False), plane_groups(shares, experts, True)
    side = len(first[0])
    side_slots = slots // side
    parts = lax.all_to_all(
        terms.reshape(side, side_slots, hidden), plane, 0, 0, tiled=True, axis_index_groups=first
    )
    partial = sum(parts[i].astype(F32) for i in range(side)).astype(WIRE)
    partial = lax.all_gather(partial, plane, axis=0, axis_index_groups=second)
    preact = sum(partial[i].astype(F32) for i in range(side)) * (1.0 / WIRE_GAIN)
    active = jax.nn.silu(preact).astype(BF16)
    active = (active.astype(F32) * ACTIVE_GAIN).astype(WIRE)
    active = lax.all_gather(active, plane, axis=0, tiled=True, axis_index_groups=first)
    own, other = (
        (rows.astype(F32) * (1.0 / ACTIVE_GAIN)).astype(BF16) for rows in jnp.split(active, 2)
    )
    own = lax.dot_general(own, down_own, NT, preferred_element_type=F32).astype(BF16)
    other = lax.dot_general(other, down_other, NT, preferred_element_type=F32).astype(BF16)
    pieces = pl.pallas_call(
        functools.partial(pack_kernel, capacity),
        out_shape=jax.ShapeDtypeStruct((chips, 2 * capacity * width // 128, 128), BF16),
        in_specs=[vmem_spec()] * 2,
        out_specs=vmem_spec(),
        compiler_params=params,
        name="pack",
    )(own, other)
    back = lax.all_to_all(pieces, "expert", 0, 0, tiled=True, axis_index_groups=rings)
    combined_t = pl.pallas_call(
        functools.partial(combine_kernel, capacity, width),
        out_shape=jax.ShapeDtypeStruct((width, tokens), F32),
        in_specs=[vmem_spec()] * 3,
        out_specs=vmem_spec(),
        compiler_params=params,
        name="combine",
    )(back, routes_t, gate_t)
    return combined_t.T


def solution(mesh):
    return jax.shard_map(
        on_device,
        mesh=mesh,
        in_specs=(
            P("expert", "pipe"),
            P("expert"),
            P("expert", None),
            P("expert", None),
            P("expert", "pipe", None),
            P("expert", None, "pipe"),
        ),
        out_specs=P("expert", "pipe"),
        check_vma=False,
    )
```
